32 devices in a mesh: tm: 2 (over core), lon: 4 (over y, x), head: 4 (over z).
Axes of the slice: x: 2, y: 2, z: 4, core: 2. Of those that a mesh axis runs over, the one named last changes fastest.
Arguments:
- query_rows: bfloat16 [8, 8, 32, 5120], P('tm', None, 'lon', 'head'), may hold values from -16 to 16
- key_rows: bfloat16 [8, 8, 32, 5120], P('tm', None, 'lon', 'head'), may hold values from -16 to 16
- value_rows: bfloat16 [8, 8, 32, 5120], P('tm', None, 'lon', 'head'), may hold values from -6 to 6
- out_grad: bfloat16 [8, 8, 32, 5120], P('tm', None, 'lon', 'head'), may hold values from -6 to 6
- window_offsets: int32 [2, 2, 8], P('tm', None, 'lon'), may hold values from -1 to 1
Outputs:
- attended: bfloat16 [8, 8, 32, 5120], P('tm', None, 'lon', 'head')
- query_grad: bfloat16 [8, 8, 32, 5120], P('tm', None, 'lon', 'head')
- key_grad: bfloat16 [8, 8, 32, 5120], P('tm', None, 'lon', 'head')
- value_grad: bfloat16 [8, 8, 32, 5120], P('tm', None, 'lon', 'head')
The draws below stay inside these ranges and needn't reach their ends.
All inputs are finite; a program needn't handle non-finite values.
Results may differ from the reference program's by a relative error of at most 0.013.
The reference program's roundings to bfloat16 on the way (of `probs` and `dscores`) count: a program that leaves them out, or rounds other values in their place, can miss the bound.
Values may be sent and summed in bfloat16 or wider, within the bound.
No kernel may reach another device: no remote copies, remote signals or barrier semaphores. Data moves between devices by JAX's collectives and lax.ppermute only.
A program may use at most 128 MiB of HBM per device.

```python
import math
import jax
import jax.numpy as jnp
from jax import lax

HEADS = 40
HD = 128
TILE = 4
LAT = 8
FRAMES = 8
LON = 32


def draw_query_rows(key, part):
    shape = (FRAMES, LAT, LON, HEADS * HD)
    noise_key = jax.random.fold_in(key, 1)
    values = jnp.clip(jax.random.normal(noise_key, shape, jnp.float32), -6.0, 6.0)
    return values.astype(jnp.bfloat16)


def draw_key_rows(key, part):
    shape = (FRAMES, LAT, LON, HEADS * HD)
    noise_key = jax.random.fold_in(key, 2)
    values = jnp.clip(jax.random.normal(noise_key, shape, jnp.float32), -6.0, 6.0)
    return values.astype(jnp.bfloat16)


def touch_ends(entries, own_key, least, high):
    dims = entries.shape
    place = [jax.random.randint(jax.random.fold_in(own_key, axis), (), 0, dims[axis]) for axis in range(len(dims))]
    entries = entries.at[tuple(place)].set(least)
    longest = dims.index(max(dims))
    place[longest] = (place[longest] + 1) % dims[longest]
    return entries.at[tuple(place)].set(high)


def level_of(stream_key, extent, pieces, least, high):
    factor_of = 1.0
    for axis_at, parts in pieces:
        draws = jax.random.uniform(jax.random.fold_in(jax.random.fold_in(stream_key, 6), axis_at), (parts,), jnp.float32, least / len(pieces), high / len(pieces))
        factor_of = factor_of * jnp.repeat(jnp.exp(draws), extent[axis_at] // parts).reshape((-1,) + (1,) * (len(extent) - 1 - axis_at))
    return factor_of


def noise(rng, extent, spread, bound, shards=(), held_as=jnp.bfloat16):
    entries = spread * jax.random.normal(rng, extent, jnp.float32)
    if shards:
        entries = entries * level_of(rng, extent, shards, -0.22, 0.18)
    return jnp.clip(entries, -bound, bound).astype(held_as)


def setup_inputs(seed: int = 0) -> dict:
    seeds = jax.random.split(jax.random.key(seed), 6)
    return {
        "query_rows": draw_query_rows(jax.random.fold_in(seeds[5], 71), 0),
        "key_rows": draw_key_rows(jax.random.fold_in(seeds[5], 71), 0),
        "value_rows": noise(seeds[2], (FRAMES, LAT, LON, HEADS * HD), 1.0, 6.0, ((0, 2), (2, 4), (3, 4))),
        "out_grad": noise(seeds[3], (FRAMES, LAT, LON, HEADS * HD), 1.0, 6.0, ((0, 2), (2, 4), (3, 4))),
        "window_offsets": touch_ends(jax.random.randint(seeds[4], (FRAMES // TILE, LAT // TILE, LON // TILE), -1, 2), jax.random.fold_in(seeds[4], 1), -1, 1).astype(jnp.int32),
    }


def reference(query_rows, key_rows, value_rows, out_grad, window_offsets):
    scale = 1.0 / math.sqrt(HD)
    frame_tiles = FRAMES // TILE
    lat_tiles = LAT // TILE
    lon_tiles = LON // TILE
    block_count = frame_tiles * lat_tiles * lon_tiles
    span = jnp.arange(3 * TILE).astype(jnp.int32)
    span_tile = (span // TILE - 1).astype(jnp.int32)
    cube = (3 * TILE, 3 * TILE, 3 * TILE)

    def to_heads(array):
        return array.reshape(FRAMES, LAT, LON, HEADS, HD).transpose(3, 0, 1, 2, 4)

    def per_head(inputs):
        query_head, key_head, value_head, grad_head = inputs

        def block(carry, index):
            key_acc, value_acc = carry
            frame_tile = (index // (lat_tiles * lon_tiles)).astype(jnp.int32)
            lat_tile = (index // lon_tiles % lat_tiles).astype(jnp.int32)
            lon_tile = (index % lon_tiles).astype(jnp.int32)
            offset = window_offsets[frame_tile, lat_tile, lon_tile].astype(jnp.int32)
            frame_index = jnp.clip(frame_tile * TILE - TILE + span, 0, FRAMES - 1).astype(jnp.int32)
            lat_index = jnp.clip(lat_tile * TILE - TILE + span, 0, LAT - 1).astype(jnp.int32)
            lon_index = (((lon_tile + offset - 1) * TILE + span) % LON).astype(jnp.int32)
            frame_ok = (frame_tile + span_tile >= 0) & (frame_tile + span_tile < frame_tiles)
            lat_ok = (lat_tile + span_tile >= 0) & (lat_tile + span_tile < lat_tiles)
            allowed = jnp.broadcast_to(frame_ok[:, None, None] & lat_ok[None, :, None], cube).reshape(-1)
            anchor = jnp.int32(0)
            corner = ((frame_tile * TILE).astype(jnp.int32), (lat_tile * TILE).astype(jnp.int32), (lon_tile * TILE).astype(jnp.int32), anchor)
            query_full = lax.dynamic_slice(query_head, corner, (TILE, TILE, TILE, HD)).astype(jnp.float32).reshape(-1, HD)
            grad_full = lax.dynamic_slice(grad_head, corner, (TILE, TILE, TILE, HD)).astype(jnp.float32).reshape(-1, HD)
            where = (frame_index[:, None, None], lat_index[None, :, None], lon_index[None, None, :])
            key_full = key_head[where].astype(jnp.float32).reshape(-1, HD)
            value_full = value_head[where].astype(jnp.float32).reshape(-1, HD)
            scores = jnp.dot(query_full, key_full.T, precision=lax.Precision.HIGHEST) * scale
            peak = lax.optimization_barrier(jnp.max(jnp.where(allowed[None, :], scores, -jnp.inf), axis=1, keepdims=True))
            expo = jnp.exp(jnp.where(allowed[None, :], scores - peak, -jnp.inf))
            probs = (expo / lax.optimization_barrier(jnp.sum(expo, axis=1, keepdims=True))).astype(jnp.bfloat16)
            probs_full = lax.optimization_barrier(probs).astype(jnp.float32)
            attended = jnp.dot(probs_full, value_full, precision=lax.Precision.HIGHEST).astype(jnp.bfloat16)
            attended_full = lax.optimization_barrier(attended).astype(jnp.float32)
            delta = lax.optimization_barrier(jnp.sum(grad_full * attended_full, axis=1, keepdims=True))
            dprobs = jnp.dot(grad_full, value_full.T, precision=lax.Precision.HIGHEST)
            dscores = (probs_full * (dprobs - delta)).astype(jnp.bfloat16)
            dscores_full = lax.optimization_barrier(dscores).astype(jnp.float32)
            query_grad = (jnp.dot(dscores_full, key_full, precision=lax.Precision.HIGHEST) * scale).astype(jnp.bfloat16)
            key_part = jnp.dot(dscores_full.T, query_full, precision=lax.Precision.HIGHEST) * scale
            value_part = jnp.dot(probs_full.T, grad_full, precision=lax.Precision.HIGHEST)
            key_acc = key_acc.at[where].add(key_part.reshape(cube + (HD,)))
            value_acc = value_acc.at[where].add(value_part.reshape(cube + (HD,)))
            return ((key_acc, value_acc), (attended, query_grad))
        zero_acc = jnp.zeros((FRAMES, LAT, LON, HD), jnp.float32)
        indices = jnp.arange(block_count).astype(jnp.int32)
        (key_acc, value_acc), (attended, query_grad) = lax.scan(block, (zero_acc, zero_acc), indices)

        def assemble(blocks):
            shaped = blocks.reshape(frame_tiles, lat_tiles, lon_tiles, TILE, TILE, TILE, HD)
            return shaped.transpose(0, 3, 1, 4, 2, 5, 6).reshape(FRAMES, LAT, LON, HD)
        return (assemble(attended), assemble(query_grad), key_acc.astype(jnp.bfloat16), value_acc.astype(jnp.bfloat16))
    results = lax.map(per_head, (to_heads(query_rows), to_heads(key_rows), to_heads(value_rows), to_heads(out_grad)))

    def from_heads(array):
        return array.transpose(1, 2, 3, 0, 4).reshape(FRAMES, LAT, LON, HEADS * HD)
    return (from_heads(results[0]), from_heads(results[1]), from_heads(results[2]), from_heads(results[3]))
```

```python
import functools
import math

import jax
import jax.numpy as jnp
from jax import lax
from jax.experimental import pallas as pl
from jax.experimental.pallas import tpu as pltpu
from jax.sharding import PartitionSpec as P

HD = 128
TILE = 4
MASKED = -1e30
CHUNKS = 2

LAST = (((1,), (1,)), ((), ()))
FIRST = (((0,), (0,)), ((), ()))
PLAIN = (((1,), (0,)), ((), ()))


def dot(a, b, dims):
    return lax.dot_general(a, b, dims, preferred_element_type=jnp.float32)


def to_partner(block):
    count = lax.axis_size("lon")
    return lax.ppermute(block, "lon", [(i, i ^ 1) for i in range(count)])


def to_far(block, outward):
    count = lax.axis_size("lon")
    route = []
    for i in range(count):
        step = 2 if (i % 2 == 0) == outward else -2
        route.append((i, (i + step) % count))
    return lax.ppermute(block, "lon", route)


def to_twin(block):
    return lax.ppermute(block, "tm", [(0, 1), (1, 0)])


def attention_kernel(
    bias_ref,
    own_q,
    par_q,
    own_a,
    own_b,
    par_a,
    par_b,
    yown_a,
    yown_b,
    rel_a,
    rel_b,
    own_out,
    par_out,
    near_ref,
    twin_ref,
    scores_ref,
    probs_ref,
    grad_ref,
):
    rows = own_q.shape[2]
    factor = math.log2(math.e) / math.sqrt(HD)
    scale = 1.0 / math.sqrt(HD)
    blocks = ((own_a, own_b), (par_a, par_b), (yown_a, yown_b), (rel_a, rel_b))
    lon = bias_ref.shape[2]
    for which, (q_ref, out_ref) in enumerate(((own_q, own_out), (par_q, par_out))):
        query = q_ref[0, 0]
        grad = q_ref[0, 1]
        used = (0, 1, 3) if which == 0 else (1, 0, 2)
        parts = [(b, f) for b in used for f in range(2)]
        peak = None
        for at, (b, f) in enumerate(parts):
            key = blocks[b][f][0, 0]
            score = dot(key, query, LAST) * factor
            score = score.reshape(rows // lon, lon, rows) + bias_ref[which, at // 2][None]
            scores_ref[at] = score.reshape(rows, rows)
            top = jnp.max(score, axis=0)
            peak = top if peak is None else jnp.maximum(peak, top)
        peak = jnp.max(peak, axis=0, keepdims=True)
        total = jnp.zeros((lon, rows), jnp.float32)
        for at in range(len(parts)):
            expo = jnp.exp2(scores_ref[at] - peak)
            scores_ref[at] = expo
            total += jnp.sum(expo.reshape(rows // lon, lon, rows), axis=0)
        inverse = 1.0 / jnp.sum(total, axis=0, keepdims=True)
        attended = jnp.zeros((HD, rows), jnp.float32)
        for at, (b, f) in enumerate(parts):
            probs = (scores_ref[at] * inverse).astype(jnp.bfloat16)
            probs_ref[at] = probs
            attended += dot(blocks[b][f][0, 1], probs, FIRST)
        attended = attended.T.astype(jnp.bfloat16)
        out_ref[0, 0] = attended
        product = grad.astype(jnp.float32) * attended.astype(jnp.float32)
        delta = jnp.sum(product.T, axis=0, keepdims=True)
        query_grad = jnp.zeros((HD, rows), jnp.float32)
        for at, (b, f) in enumerate(parts):
            key = blocks[b][f][0, 0]
            value = blocks[b][f][0, 1]
            probs = probs_ref[at]
            dprobs = dot(value, grad, LAST)
            dscores = (probs.astype(jnp.float32) * (dprobs - delta)).astype(jnp.bfloat16)
            query_grad += dot(key, dscores, FIRST)
            key_part = dot(dscores, query, PLAIN) * scale
            value_part = dot(probs, grad, PLAIN)
            if which == 0 and b != 2 or b == 2:
                grad_ref[b, f, 0] = key_part
                grad_ref[b, f, 1] = value_part
            else:
                grad_ref[b, f, 0] += key_part
                grad_ref[b, f, 1] += value_part
        out_ref[0, 1] = (query_grad * scale).T.astype(jnp.bfloat16)
    for b in range(4):
        near_ref[0, b] = grad_ref[b, 0]
        twin_ref[0, b] = grad_ref[b, 1].astype(jnp.bfloat16)


def attention(bias, own_q, par_q, blocks):
    heads, _, rows, _ = own_q.shape
    one = pl.BlockSpec((1, 2, rows, HD), lambda h: (h, 0, 0, 0))
    whole = pl.BlockSpec(bias.shape, lambda h: (0, 0, 0, 0))
    flat = [part for pair in blocks for part in pair]
    pairs = (heads, 2, rows, HD)
    spread = (heads, 4, 2, rows, HD)
    per_head = pl.BlockSpec((1, 4, 2, rows, HD), lambda h: (h, 0, 0, 0, 0))
    work = heads * 2 * 6 * 6 * 2 * rows * rows * HD
    return pl.pallas_call(
        attention_kernel,
        grid=(heads,),
        in_specs=[whole] + [one] * (2 + len(flat)),
        out_specs=[one, one, per_head, per_head],
        out_shape=[
            jax.ShapeDtypeStruct(pairs, jnp.bfloat16),
            jax.ShapeDtypeStruct(pairs, jnp.bfloat16),
            jax.ShapeDtypeStruct(spread, jnp.float32),
            jax.ShapeDtypeStruct(spread, jnp.bfloat16),
        ],
        scratch_shapes=[
            pltpu.VMEM((6, rows, rows), jnp.float32),
            pltpu.VMEM((6, rows, rows), jnp.bfloat16),
            pltpu.VMEM((4, 2, 2, rows, HD), jnp.float32),
        ],
        compiler_params=pltpu.CompilerParams(vmem_limit_bytes=40 * 1024 * 1024),
        cost_estimate=pl.CostEstimate(
            flops=work, bytes_accessed=heads * 28 * rows * HD * 2, transcendentals=heads * 12 * rows * rows
        ),
        name="attention",
    )(bias, own_q, par_q, *flat)


def window_bias(offsets, side, frames, lats, lons):
    lat_tiles, lon_tiles = offsets.shape[1:]
    per_row = jnp.repeat(jnp.repeat(offsets, TILE, axis=1), TILE, axis=2)
    centre = per_row + (jnp.arange(lons) // TILE)[None, None, :]
    centre = jnp.broadcast_to(centre[:, None], (2, frames, lats, lons)).reshape(2, -1)
    sign = 1 - 2 * side
    place = jnp.arange(lons) // TILE
    shift = jnp.array([[0, 1, -1], [0, -1, 1]], jnp.int32) * sign * lon_tiles
    column = shift[:, :, None] + place[None, None, :]
    near = jnp.abs(column[:, :, :, None] - centre[:, None, None, :]) <= 1
    return jnp.where(near, 0.0, MASKED).astype(jnp.float32)


def on_device(query_rows, key_rows, value_rows, out_grad, window_offsets):
    frames, lats, lons, width = query_rows.shape
    heads = width // HD
    half = heads // 2
    rows = frames * lats * lons
    frame_tiles = frames // TILE * lax.axis_size("tm")
    if frame_tiles > 2 or lats // TILE > 2 or lons != 2 * TILE or heads % 2:
        raise ValueError("unsupported block")
    side = lax.axis_index("lon") % 2

    def by_head(first, second):
        pair = jnp.stack([first, second]).reshape(2, frames, lats, lons, heads, HD)
        return pair.transpose(4, 0, 1, 2, 3, 5).reshape(heads, 2, rows, HD)

    key_value = by_head(key_rows, value_rows)
    query_grad = by_head(query_rows, out_grad)

    def halves(array):
        mine = lax.dynamic_slice_in_dim(array, side * half, half, 0)
        theirs = lax.dynamic_slice_in_dim(array, (1 - side) * half, half, 0)
        return mine, theirs

    mine_kv, theirs_kv = halves(key_value)
    mine_qg, theirs_qg = halves(query_grad)
    offsets = window_offsets.reshape(lats // TILE, lons // TILE)
    bias = window_bias(jnp.stack([offsets, to_partner(offsets)]), side, frames, lats, lons)

    bounds = [half * c // CHUNKS for c in range(CHUNKS + 1)]
    spans = list(zip(bounds[:-1], bounds[1:]))
    results = []
    for low, high in spans:
        own = mine_kv[low:high]
        partner = to_partner(theirs_kv[low:high])
        far = to_far(own, False)
        partner_q = to_partner(theirs_qg[low:high])
        relayed = to_far(partner, True)
        blocks = [(part, to_twin(part)) for part in (own, partner, far, relayed)]
        own_out, partner_out, near, twin = attention(bias, mine_qg[low:high], partner_q, blocks)
        summed = near + to_twin(twin).astype(jnp.float32)
        back_out = to_partner(partner_out)
        back_relay = to_far(summed[:, 3].astype(jnp.bfloat16), False)
        back_far = to_far(summed[:, 2].astype(jnp.bfloat16), True)
        theirs_grad = to_partner((summed[:, 1] + back_relay.astype(jnp.float32)).astype(jnp.bfloat16))
        mine_grad = (summed[:, 0] + back_far.astype(jnp.float32)).astype(jnp.bfloat16)
        results.append((own_out, mine_grad, back_out, theirs_grad))

    own_out, mine_grad, back_out, theirs_grad = (jnp.concatenate(r) for r in zip(*results))

    def assembled(mine, theirs):
        low = jnp.where(side == 0, mine, theirs)
        high = jnp.where(side == 0, theirs, mine)
        array = jnp.concatenate([low, high])
        shaped = array.reshape(heads, 2, frames, lats, lons, HD).transpose(1, 2, 3, 4, 0, 5)
        shaped = shaped.reshape(2, frames, lats, lons, width)
        return shaped[0], shaped[1]

    attended, query_out = assembled(own_out, back_out)
    key_out, value_out = assembled(mine_grad, theirs_grad)
    return attended, query_out, key_out, value_out


def solution(mesh):
    rows = P("tm", None, "lon", "head")
    return jax.shard_map(
        on_device,
        mesh=mesh,
        in_specs=(rows, rows, rows, rows, P("tm", None, "lon")),
        out_specs=(rows, rows, rows, rows),
        check_vma=False,
    )
```

```python
import math

import jax
import jax.numpy as jnp
from jax import lax
from jax.experimental import pallas as pl
from jax.experimental.pallas import tpu as pltpu
from jax.sharding import PartitionSpec as P

HD = 128
TILE = 4
MASKED = -1e30
FIRST_HEADS = 2
LAST_HEADS = 1

LAST = (((1,), (1,)), ((), ()))
FIRST = (((0,), (0,)), ((), ()))
PLAIN = (((1,), (0,)), ((), ()))


def dot(a, b, dims):
    return lax.dot_general(a, b, dims, preferred_element_type=jnp.float32)


def to_partner(block):
    count = lax.axis_size("lon")
    return lax.ppermute(block, "lon", [(i, i ^ 1) for i in range(count)])


def to_far(block, outward):
    count = lax.axis_size("lon")
    route = []
    for i in range(count):
        step = 2 if (i % 2 == 0) == outward else -2
        route.append((i, (i + step) % count))
    return lax.ppermute(block, "lon", route)


def to_twin(block):
    return lax.ppermute(block, "tm", [(0, 1), (1, 0)])


class Order:
    def __init__(self):
        self.token = jnp.zeros((), jnp.float32)

    def gate(self, value):
        return lax.optimization_barrier((self.token, value))[1]

    def passed(self, *values):
        self.token, *values = lax.optimization_barrier((self.token, *values))
        return values if len(values) > 1 else values[0]


def attention_kernel(
    bias_ref,
    own_q,
    par_q,
    own_a,
    own_b,
    par_a,
    par_b,
    yown_a,
    yown_b,
    rel_a,
    rel_b,
    own_out,
    par_out,
    near_own,
    near_par,
    near_far,
    near_rel,
    twin_stay,
    twin_send,
    key_ref,
    value_ref,
    scores_ref,
    probs_ref,
    dprobs_ref,
    grad_ref,
):
    rows = own_q.shape[2]
    lon = bias_ref.shape[2]
    scale = 1.0 / math.sqrt(HD)
    factor = math.log2(math.e) * scale
    ring = (rel_a, rel_b, own_a, own_b, par_a, par_b, yown_a, yown_b)
    for at, ref in enumerate(ring):
        key_ref[at] = ref[0, 0]
        value_ref[at] = ref[0, 1]
    span = 6
    for which, (q_ref, out_ref) in enumerate(((own_q, own_out), (par_q, par_out))):
        first = 2 * which
        query = q_ref[0, 0]
        grad = q_ref[0, 1]
        peak = None
        for at in range(span):
            score = dot(key_ref[first + at], query, LAST)
            score = score.reshape(rows // lon, lon, rows) + bias_ref[which, at // 2][None]
            scores_ref[at] = score.reshape(rows, rows)
            top = jnp.max(score, axis=0)
            peak = top if peak is None else jnp.maximum(peak, top)
        peak = jnp.max(peak, axis=0, keepdims=True)
        total = jnp.zeros((lon, rows), jnp.float32)
        attended = jnp.zeros((HD, rows), jnp.float32)
        for at in range(span):
            expo = jnp.exp2((scores_ref[at] - peak) * factor)
            total += jnp.sum(expo.reshape(rows // lon, lon, rows), axis=0)
            probs = expo.astype(jnp.bfloat16)
            probs_ref[at] = probs
            attended += dot(value_ref[first + at], probs, FIRST)
            dprobs_ref[at] = dot(value_ref[first + at], grad, LAST)
        inverse = 1.0 / jnp.sum(total, axis=0, keepdims=True)
        column = jnp.broadcast_to(inverse, (HD, rows)).T
        query_part = (query.astype(jnp.float32) * (column * scale)).astype(jnp.bfloat16)
        grad_part = (grad.astype(jnp.float32) * column).astype(jnp.bfloat16)
        attended = (attended * inverse).astype(jnp.bfloat16)
        out_ref[0, 0] = attended.T
        product = grad.T.astype(jnp.float32) * attended.astype(jnp.float32)
        delta = jnp.sum(product, axis=0, keepdims=True)
        query_grad = jnp.zeros((HD, rows), jnp.float32)
        for at in range(span):
            probs = probs_ref[at]
            dscores = probs.astype(jnp.float32) * (dprobs_ref[at] - delta)
            dscores = dscores.astype(jnp.bfloat16)
            query_grad += dot(key_ref[first + at], dscores, FIRST)
            key_part = dot(dscores, query_part, PLAIN)
            value_part = dot(probs, grad_part, PLAIN)
            if which == 0 or at >= 4:
                grad_ref[first + at, 0] = key_part
                grad_ref[first + at, 1] = value_part
            else:
                grad_ref[first + at, 0] += key_part
                grad_ref[first + at, 1] += value_part
        out_ref[0, 1] = (query_grad * (inverse * scale)).T.astype(jnp.bfloat16)
    for b, (at, near_ref) in enumerate(((2, near_own), (4, near_par), (6, near_far), (0, near_rel))):
        near_ref[0] = grad_ref[at].astype(jnp.bfloat16)
        twin_ref = twin_stay if b < 2 else twin_send
        twin_ref[b % 2, 0] = grad_ref[at + 1].astype(jnp.bfloat16)


def attention(bias, own_q, partner_q, blocks, low, skip, heads):
    rows = own_q.shape[2]
    here = pl.BlockSpec((1, 2, rows, HD), lambda h: (h + low, 0, 0, 0))
    there = pl.BlockSpec((1, 2, rows, HD), lambda h: (h + skip, 0, 0, 0))
    one = pl.BlockSpec((1, 2, rows, HD), lambda h: (h, 0, 0, 0))
    whole = pl.BlockSpec(bias.shape, lambda h: (0, 0, 0, 0))
    flat = [part for pair in blocks for part in pair]
    pairs = (heads, 2, rows, HD)
    spread = (2, heads, 2, rows, HD)
    per_head = pl.BlockSpec((2, 1, 2, rows, HD), lambda h: (0, h, 0, 0, 0))
    operands = [pltpu.with_memory_space_constraint(x, pltpu.HBM) for x in (own_q, partner_q, *flat[:-1])]
    operands.append(pltpu.with_memory_space_constraint(flat[-1], pltpu.VMEM))
    return pl.pallas_call(
        attention_kernel,
        grid=(heads,),
        in_specs=[whole, here, there, here, here, there, there, here, here, there, there],
        out_specs=[one] * 6 + [per_head] * 2,
        out_shape=[
            pltpu.HBM(shape, jnp.bfloat16) for shape in [pairs] * 6 + [spread] * 2
        ],
        scratch_shapes=[
            pltpu.VMEM((8, rows, HD), jnp.bfloat16),
            pltpu.VMEM((8, rows, HD), jnp.bfloat16),
            pltpu.VMEM((6, rows, rows), jnp.float32),
            pltpu.VMEM((6, rows, rows), jnp.bfloat16),
            pltpu.VMEM((6, rows, rows), jnp.float32),
            pltpu.VMEM((8, 2, rows, HD), jnp.float32),
        ],
        compiler_params=pltpu.CompilerParams(vmem_limit_bytes=18 * 1024 * 1024),
        cost_estimate=pl.CostEstimate(
            flops=heads * 2 * 6 * 6 * 2 * rows * rows * HD, bytes_accessed=heads * 28 * rows * HD * 2, transcendentals=0
        ),
        name="attention",
    )(bias, *operands)


def window_bias(offsets, side, frames, lats, lons):
    lat_tiles, lon_tiles = offsets.shape[1:]
    per_row = jnp.repeat(jnp.repeat(offsets, TILE, axis=1), TILE, axis=2)
    centre = per_row + (jnp.arange(lons) // TILE)[None, None, :]
    centre = jnp.broadcast_to(centre[:, None], (2, frames, lats, lons)).reshape(2, -1)
    sign = 1 - 2 * side
    place = jnp.arange(lons) // TILE
    shift = jnp.array([[-1, 0, 1], [-1, 0, 1]], jnp.int32) * sign * lon_tiles
    column = shift[:, :, None] + place[None, None, :]
    near = jnp.abs(column[:, :, :, None] - centre[:, None, None, :]) <= 1
    return jnp.where(near, 0.0, MASKED).astype(jnp.float32)


def on_device(query_rows, key_rows, value_rows, out_grad, window_offsets):
    frames, lats, lons, width = query_rows.shape
    heads = width // HD
    half = heads // 2
    rows = frames * lats * lons
    frame_tiles = frames // TILE * lax.axis_size("tm")
    if lax.axis_size("tm") != 2 or frame_tiles > 2 or lats // TILE > 2 or lons != 2 * TILE or heads % 2:
        raise ValueError("unsupported block")
    side = lax.axis_index("lon") % 2

    def by_head(*arrays):
        pair = jnp.stack(arrays).reshape(len(arrays), frames, lats, lons, heads, HD)
        return pair.transpose(4, 0, 1, 2, 3, 5).reshape(heads, len(arrays), rows, HD)

    def half_of(array, which):
        return lax.dynamic_slice_in_dim(array, which * half, half, 0)

    key_value = by_head(key_rows, value_rows)
    mine_kv, theirs_kv = half_of(key_value, side), half_of(key_value, 1 - side)
    query_grad = by_head(query_rows, out_grad)
    mine_qg, theirs_qg = half_of(query_grad, side), half_of(query_grad, 1 - side)
    offsets = window_offsets.reshape(lats // TILE, lons // TILE)

    first = min(FIRST_HEADS, half - 1)
    last = half - min(LAST_HEADS, half - first)
    order = Order()
    far = to_far(mine_kv, False)
    partner_0 = to_partner(theirs_kv[:first])
    both = to_partner(order.gate(offsets))
    partner_1 = to_partner(theirs_kv[first:])
    own_b = to_twin(mine_kv)
    partner_0 = order.passed(partner_0)
    relay_0 = to_far(order.gate(partner_0), True)
    part_q0 = to_partner(order.gate(theirs_qg[:first]))
    relay_0, part_q0, far, partner_1, both, own_b = order.passed(relay_0, part_q0, far, partner_1, both, own_b)
    bias = window_bias(jnp.stack([offsets, both]), side, frames, lats, lons)
    relay_0b = to_twin(order.gate(relay_0))
    far_b = to_twin(order.gate(far))
    partner_0b = to_twin(order.gate(partner_0))
    relay_1 = to_far(order.gate(partner_1), True)
    part_q1 = to_partner(order.gate(theirs_qg[first:]))
    relay_0b, partner_0b, far_b = order.passed(relay_0b, partner_0b, far_b)
    partner_1b = to_twin(order.gate(partner_1))

    def compute(low, high, partner, relay, part_q):
        skip = low - (first if low else 0)
        blocks = [(mine_kv, own_b), partner, (far, far_b), relay]
        return attention(order.gate(bias), mine_qg, part_q, blocks, low, skip, high - low)

    def total(near, twin, block):
        return near[block] + twin[block % 2].astype(jnp.float32)

    def rounded(near, twin, block):
        return total(near, twin, block).astype(jnp.bfloat16)

    def theirs_total(near, twin, back):
        return (total(near, twin, 1) + back.astype(jnp.float32)).astype(jnp.bfloat16)

    def send_back(near, twin):
        relayed, ahead = rounded(near, twin, 3), rounded(near, twin, 2)
        if lax.axis_size("lon") == 4:
            return to_far(jnp.stack([relayed, ahead]), True)
        return to_far(relayed, False), to_far(ahead, True)

    done_0, out_0, *near_0, stay_0, send_0 = compute(
        0, first, (partner_0, partner_0b), (relay_0, relay_0b), part_q0
    )
    send_0, relay_1, part_q1, partner_1b = order.passed(send_0, relay_1, part_q1, partner_1b)
    send_0 = to_twin(order.gate(send_0))
    relay_1b = to_twin(order.gate(relay_1))
    send_0, relay_1b = order.passed(send_0, relay_1b)
    back_0, ahead_0 = send_back(near_0, send_0)
    back_out_0 = to_partner(order.gate(out_0))
    stay_0 = to_twin(order.gate(stay_0))

    rest = (partner_1, partner_1b), (relay_1, relay_1b), part_q1
    done_1, out_1, *near_1, stay_1, send_1 = compute(first, last, *rest)
    send_1, back_0, ahead_0, back_out_0, stay_0 = order.passed(send_1, back_0, ahead_0, back_out_0, stay_0)
    send_1 = to_twin(order.gate(send_1))
    theirs_0 = theirs_total(near_0, stay_0, order.gate(back_0))
    mixed_1 = to_partner(jnp.concatenate([theirs_0, order.gate(out_1)]))
    send_1 = order.passed(send_1)
    back_1, ahead_1 = send_back(near_1, send_1)
    stay_1 = to_twin(order.gate(stay_1))

    done_2, out_2, *near_2, stay_2, send_2 = compute(last, half, *rest)
    send_2 = order.passed(send_2)
    send_2 = to_twin(order.gate(send_2))
    send_2, back_1, ahead_1, mixed_1, stay_1 = order.passed(send_2, back_1, ahead_1, mixed_1, stay_1)
    back_2 = to_far(rounded(near_2, send_2, 3), False)
    theirs_1 = theirs_total(near_1, stay_1, order.gate(back_1))
    mixed_2 = to_partner(jnp.concatenate([theirs_1, order.gate(out_2)]))
    stay_2 = to_twin(order.gate(stay_2))
    back_2, stay_2 = order.passed(back_2, stay_2)
    theirs_2 = to_partner(theirs_total(near_2, stay_2, order.gate(back_2)))
    ahead_2 = to_far(order.gate(rounded(near_2, send_2, 2)), True)

    theirs_0, back_out_1 = mixed_1[:first], mixed_1[first:]
    theirs_1, back_out_2 = mixed_2[: last - first], mixed_2[last - first :]
    def assembled(mine, theirs):
        mine, theirs = jnp.concatenate(mine), jnp.concatenate(theirs)
        low = jnp.where(side == 0, mine, theirs)
        high = jnp.where(side == 0, theirs, mine)
        array = jnp.concatenate([low, high])
        shaped = array.reshape(heads, 2, frames, lats, lons, HD).transpose(1, 2, 3, 4, 0, 5)
        shaped = shaped.reshape(2, frames, lats, lons, width)
        return shaped[0], shaped[1]

    attended, query_out = assembled((done_0, done_1, done_2), (back_out_0, back_out_1, back_out_2))
    theirs_2, ahead_2, attended, query_out = order.passed(theirs_2, ahead_2, attended, query_out)
    mine = [
        (total(near, twin, 0) + ahead.astype(jnp.float32)).astype(jnp.bfloat16)
        for near, twin, ahead in ((near_0, stay_0, ahead_0), (near_1, stay_1, ahead_1), (near_2, stay_2, ahead_2))
    ]
    key_out, value_out = assembled(mine, (theirs_0, theirs_1, theirs_2))
    return attended, query_out, key_out, value_out


def solution(mesh):
    rows = P("tm", None, "lon", "head")
    return jax.shard_map(
        on_device,
        mesh=mesh,
        in_specs=(rows, rows, rows, rows, P("tm", None, "lon")),
        out_specs=(rows, rows, rows, rows),
        check_vma=False,
    )
```

```python
import math

import jax
import jax.numpy as jnp
from jax import lax
from jax.experimental import pallas as pl
from jax.experimental.pallas import tpu as pltpu
from jax.sharding import PartitionSpec as P

HD = 128
TILE = 4
MASKED = -1e30
FIRST_HEADS = 2
LAST_HEADS = 1

LAST = (((1,), (1,)), ((), ()))
FIRST = (((0,), (0,)), ((), ()))
PLAIN = (((1,), (0,)), ((), ()))


def dot(a, b, dims):
    return lax.dot_general(a, b, dims, preferred_element_type=jnp.float32)


def to_partner(block):
    count = lax.axis_size("lon")
    return lax.ppermute(block, "lon", [(i, i ^ 1) for i in range(count)])


def to_far(block, outward):
    count = lax.axis_size("lon")
    route = []
    for i in range(count):
        step = 2 if (i % 2 == 0) == outward else -2
        route.append((i, (i + step) % count))
    return lax.ppermute(block, "lon", route)


def to_twin(block):
    return lax.ppermute(block, "tm", [(0, 1), (1, 0)])


class Order:
    def __init__(self):
        self.token = jnp.zeros((), jnp.float32)

    def gate(self, value):
        return lax.optimization_barrier((self.token, value))[1]

    def passed(self, *values):
        self.token, *values = lax.optimization_barrier((self.token, *values))
        return values if len(values) > 1 else values[0]


def attention_kernel(
    bias_ref,
    own_q,
    par_q,
    own_a,
    own_b,
    par_a,
    par_b,
    yown_a,
    yown_b,
    rel_a,
    rel_b,
    own_out,
    par_out,
    near_own,
    near_par,
    near_far,
    near_rel,
    twin_stay,
    twin_send,
    scores_ref,
    probs_ref,
    dprobs_ref,
    grad_ref,
):
    rows = own_q.shape[2]
    lon = bias_ref.shape[2]
    scale = 1.0 / math.sqrt(HD)
    factor = math.log2(math.e) * scale
    ring = (rel_a, rel_b, own_a, own_b, par_a, par_b, yown_a, yown_b)
    span = 6
    sides = ((own_q, own_out), (par_q, par_out))
    peaks, totals, outs, deltas, query_grads, parts = ([None, None] for _ in range(6))

    def score_step(which, at):
        score = dot(ring[2 * which + at][0, 0], sides[which][0][0, 0], LAST)
        score = score.reshape(rows // lon, lon, rows) + bias_ref[which, at // 2][None]
        scores_ref[which, at] = score.reshape(rows, rows)
        top = jnp.max(score, axis=0)
        peaks[which] = top if at == 0 else jnp.maximum(peaks[which], top)

    def peak_done(which):
        peaks[which] = jnp.max(peaks[which], axis=0, keepdims=True)
        totals[which] = jnp.zeros((lon, rows), jnp.float32)
        outs[which] = jnp.zeros((HD, rows), jnp.float32)

    def probs_step(which, at):
        expo = jnp.exp2((scores_ref[which, at] - peaks[which]) * factor)
        totals[which] += jnp.sum(expo.reshape(rows // lon, lon, rows), axis=0)
        probs = expo.astype(jnp.bfloat16)
        probs_ref[which, at] = probs
        value = ring[2 * which + at][0, 1]
        outs[which] += dot(value, probs, FIRST)
        dprobs_ref[which, at] = dot(value, sides[which][0][0, 1], LAST)

    def probs_done(which):
        query, grad = sides[which][0][0, 0], sides[which][0][0, 1]
        inverse = 1.0 / jnp.sum(totals[which], axis=0, keepdims=True)
        totals[which] = inverse
        column = jnp.broadcast_to(inverse, (HD, rows)).T
        parts[which] = (
            (query.astype(jnp.float32) * (column * scale)).astype(jnp.bfloat16),
            (grad.astype(jnp.float32) * column).astype(jnp.bfloat16),
        )
        attended = (outs[which] * inverse).astype(jnp.bfloat16)
        sides[which][1][0, 0] = attended.T
        product = grad.T.astype(jnp.float32) * attended.astype(jnp.float32)
        deltas[which] = jnp.sum(product, axis=0, keepdims=True)
        query_grads[which] = jnp.zeros((HD, rows), jnp.float32)

    def grad_step(which, at):
        place = 2 * which + at
        probs = probs_ref[which, at]
        dscores = probs.astype(jnp.float32) * (dprobs_ref[which, at] - deltas[which])
        dscores = dscores.astype(jnp.bfloat16)
        query_grads[which] += dot(ring[place][0, 0], dscores, FIRST)
        key_part = dot(dscores, parts[which][0], PLAIN)
        value_part = dot(probs, parts[which][1], PLAIN)
        if which == 0 or at >= 4:
            grad_ref[place, 0] = key_part
            grad_ref[place, 1] = value_part
        else:
            grad_ref[place, 0] += key_part
            grad_ref[place, 1] += value_part

    def grad_done(which):
        sides[which][1][0, 1] = (query_grads[which] * (totals[which] * scale)).T.astype(jnp.bfloat16)

    for at in range(span):
        score_step(0, at)
    peak_done(0)
    for at in range(span):
        probs_step(0, at)
        score_step(1, at)
    probs_done(0)
    peak_done(1)
    for at in range(span):
        grad_step(0, at)
        probs_step(1, at)
    grad_done(0)
    probs_done(1)
    for at in range(span):
        grad_step(1, at)
    grad_done(1)
    for b, (at, near_ref) in enumerate(((2, near_own), (4, near_par), (6, near_far), (0, near_rel))):
        near_ref[0] = grad_ref[at].astype(jnp.bfloat16)
        twin_ref = twin_stay if b < 2 else twin_send
        twin_ref[b % 2, 0] = grad_ref[at + 1].astype(jnp.bfloat16)


def attention(bias, own_q, partner_q, blocks, low, skip, heads):
    rows = own_q.shape[2]
    here = pl.BlockSpec((1, 2, rows, HD), lambda h: (h + low, 0, 0, 0))
    there = pl.BlockSpec((1, 2, rows, HD), lambda h: (h + skip, 0, 0, 0))
    one = pl.BlockSpec((1, 2, rows, HD), lambda h: (h, 0, 0, 0))
    whole = pl.BlockSpec(bias.shape, lambda h: (0, 0, 0, 0))
    flat = [part for pair in blocks for part in pair]
    pairs = (heads, 2, rows, HD)
    spread = (2, heads, 2, rows, HD)
    per_head = pl.BlockSpec((2, 1, 2, rows, HD), lambda h: (0, h, 0, 0, 0))
    operands = [pltpu.with_memory_space_constraint(x, pltpu.HBM) for x in (own_q, partner_q, *flat[:-1])]
    operands.append(pltpu.with_memory_space_constraint(flat[-1], pltpu.VMEM))
    return pl.pallas_call(
        attention_kernel,
        grid=(heads,),
        in_specs=[whole, here, there, here, here, there, there, here, here, there, there],
        out_specs=[one] * 6 + [per_head] * 2,
        out_shape=[
            pltpu.HBM(shape, jnp.bfloat16) for shape in [pairs] * 6 + [spread] * 2
        ],
        scratch_shapes=[
            pltpu.VMEM((2, 6, rows, rows), jnp.float32),
            pltpu.VMEM((2, 6, rows, rows), jnp.bfloat16),
            pltpu.VMEM((2, 6, rows, rows), jnp.float32),
            pltpu.VMEM((8, 2, rows, HD), jnp.float32),
        ],
        compiler_params=pltpu.CompilerParams(vmem_limit_bytes=26 * 1024 * 1024),
        cost_estimate=pl.CostEstimate(
            flops=heads * 2 * 6 * 6 * 2 * rows * rows * HD, bytes_accessed=heads * 28 * rows * HD * 2, transcendentals=0
        ),
        name="attention",
    )(bias, *operands)


def window_bias(offsets, side, frames, lats, lons):
    lat_tiles, lon_tiles = offsets.shape[1:]
    per_row = jnp.repeat(jnp.repeat(offsets, TILE, axis=1), TILE, axis=2)
    centre = per_row + (jnp.arange(lons) // TILE)[None, None, :]
    centre = jnp.broadcast_to(centre[:, None], (2, frames, lats, lons)).reshape(2, -1)
    sign = 1 - 2 * side
    place = jnp.arange(lons) // TILE
    shift = jnp.array([[-1, 0, 1], [-1, 0, 1]], jnp.int32) * sign * lon_tiles
    column = shift[:, :, None] + place[None, None, :]
    near = jnp.abs(column[:, :, :, None] - centre[:, None, None, :]) <= 1
    return jnp.where(near, 0.0, MASKED).astype(jnp.float32)


def on_device(query_rows, key_rows, value_rows, out_grad, window_offsets):
    frames, lats, lons, width = query_rows.shape
    heads = width // HD
    half = heads // 2
    rows = frames * lats * lons
    frame_tiles = frames // TILE * lax.axis_size("tm")
    if lax.axis_size("tm") != 2 or frame_tiles > 2 or lats // TILE > 2 or lons != 2 * TILE or heads % 2:
        raise ValueError("unsupported block")
    side = lax.axis_index("lon") % 2

    def by_head(*arrays):
        pair = jnp.stack(arrays).reshape(len(arrays), frames, lats, lons, heads, HD)
        return pair.transpose(4, 0, 1, 2, 3, 5).reshape(heads, len(arrays), rows, HD)

    def half_of(array, which):
        return lax.dynamic_slice_in_dim(array, which * half, half, 0)

    key_value = by_head(key_rows, value_rows)
    mine_kv, theirs_kv = half_of(key_value, side), half_of(key_value, 1 - side)
    query_grad = by_head(query_rows, out_grad)
    mine_qg, theirs_qg = half_of(query_grad, side), half_of(query_grad, 1 - side)
    offsets = window_offsets.reshape(lats // TILE, lons // TILE)

    first = min(FIRST_HEADS, half - 1)
    last = half - min(LAST_HEADS, half - first)
    order = Order()
    far = to_far(mine_kv, False)
    partner_0 = to_partner(theirs_kv[:first])
    both = to_partner(order.gate(offsets))
    partner_1 = to_partner(theirs_kv[first:])
    own_b = to_twin(mine_kv)
    partner_0 = order.passed(partner_0)
    relay_0 = to_far(order.gate(partner_0), True)
    part_q0 = to_partner(order.gate(theirs_qg[:first]))
    relay_0, part_q0, far, partner_1, both, own_b = order.passed(relay_0, part_q0, far, partner_1, both, own_b)
    bias = window_bias(jnp.stack([offsets, both]), side, frames, lats, lons)
    relay_0b = to_twin(order.gate(relay_0))
    far_b = to_twin(order.gate(far))
    partner_0b = to_twin(order.gate(partner_0))
    relay_1 = to_far(order.gate(partner_1), True)
    part_q1 = to_partner(order.gate(theirs_qg[first:]))
    relay_0b, partner_0b, far_b = order.passed(relay_0b, partner_0b, far_b)
    partner_1b = to_twin(order.gate(partner_1))

    def compute(low, high, partner, relay, part_q):
        skip = low - (first if low else 0)
        blocks = [(mine_kv, own_b), partner, (far, far_b), relay]
        return attention(order.gate(bias), mine_qg, part_q, blocks, low, skip, high - low)

    def total(near, twin, block):
        return near[block] + twin[block % 2].astype(jnp.float32)

    def rounded(near, twin, block):
        return total(near, twin, block).astype(jnp.bfloat16)

    def theirs_total(near, twin, back):
        return (total(near, twin, 1) + back.astype(jnp.float32)).astype(jnp.bfloat16)

    done_0, out_0, *near_0, stay_0, send_0 = compute(
        0, first, (partner_0, partner_0b), (relay_0, relay_0b), part_q0
    )
    send_0, relay_1, part_q1, partner_1b = order.passed(send_0, relay_1, part_q1, partner_1b)
    send_0 = to_twin(order.gate(send_0))
    relay_1b = to_twin(order.gate(relay_1))
    send_0, relay_1b = order.passed(send_0, relay_1b)
    back_0 = to_far(rounded(near_0, send_0, 3), False)
    back_out_0 = to_partner(order.gate(out_0))
    stay_0 = to_twin(order.gate(stay_0))

    rest = (partner_1, partner_1b), (relay_1, relay_1b), part_q1
    done_1, out_1, *near_1, stay_1, send_1 = compute(first, last, *rest)
    send_1, back_0, back_out_0, stay_0 = order.passed(send_1, back_0, back_out_0, stay_0)
    send_1 = to_twin(order.gate(send_1))
    theirs_0 = theirs_total(near_0, stay_0, order.gate(back_0))
    mixed_1 = to_partner(jnp.concatenate([theirs_0, order.gate(out_1)]))
    send_1 = order.passed(send_1)
    back_1 = to_far(rounded(near_1, send_1, 3), False)
    ahead_0 = to_far(order.gate(rounded(near_0, send_0, 2)), True)
    stay_1 = to_twin(order.gate(stay_1))

    done_2, out_2, *near_2, stay_2, send_2 = compute(last, half, *rest)
    send_2, back_1, stay_1 = order.passed(send_2, back_1, stay_1)
    send_2 = to_twin(order.gate(send_2))
    theirs_1 = theirs_total(near_1, stay_1, order.gate(back_1))
    payload = jnp.concatenate([theirs_1, order.gate(out_2)])
    send_2 = order.passed(send_2)
    outward = rounded(near_2, send_2, 3)
    outward, payload, mixed_1, ahead_0 = order.passed(outward, payload, mixed_1, ahead_0)
    back_2 = to_far(outward, False)
    mixed_2 = to_partner(payload)
    stay_2 = to_twin(order.gate(stay_2))
    back_2, stay_2 = order.passed(back_2, stay_2)
    theirs_2 = to_partner(theirs_total(near_2, stay_2, order.gate(back_2)))
    ahead_12 = to_far(order.gate(jnp.concatenate([rounded(near_1, send_1, 2), rounded(near_2, send_2, 2)])), True)

    theirs_0, back_out_1 = mixed_1[:first], mixed_1[first:]
    theirs_1, back_out_2 = mixed_2[: last - first], mixed_2[last - first :]
    def assembled(mine, theirs):
        mine, theirs = jnp.concatenate(mine), jnp.concatenate(theirs)
        low = jnp.where(side == 0, mine, theirs)
        high = jnp.where(side == 0, theirs, mine)
        array = jnp.concatenate([low, high])
        shaped = array.reshape(heads, 2, frames, lats, lons, HD).transpose(1, 2, 3, 4, 0, 5)
        shaped = shaped.reshape(2, frames, lats, lons, width)
        return shaped[0], shaped[1]

    attended, query_out = assembled((done_0, done_1, done_2), (back_out_0, back_out_1, back_out_2))
    theirs_2, ahead_12, attended, query_out = order.passed(theirs_2, ahead_12, attended, query_out)
    ahead_1, ahead_2 = ahead_12[: last - first], ahead_12[last - first :]
    mine = [
        (total(near, twin, 0) + ahead.astype(jnp.float32)).astype(jnp.bfloat16)
        for near, twin, ahead in ((near_0, stay_0, ahead_0), (near_1, stay_1, ahead_1), (near_2, stay_2, ahead_2))
    ]
    key_out, value_out = assembled(mine, (theirs_0, theirs_1, theirs_2))
    return attended, query_out, key_out, value_out


def solution(mesh):
    rows = P("tm", None, "lon", "head")
    return jax.shard_map(
        on_device,
        mesh=mesh,
        in_specs=(rows, rows, rows, rows, P("tm", None, "lon")),
        out_specs=(rows, rows, rows, rows),
        check_vma=False,
    )
```

```python
import math

import jax
import jax.numpy as jnp
from jax import lax
from jax.experimental import pallas as pl
from jax.experimental.pallas import tpu as pltpu
from jax.sharding import PartitionSpec as P

HD = 128
TILE = 4
MASKED = -1e30
FIRST_HEADS = 2
LAST_HEADS = 1

LAST = (((1,), (1,)), ((), ()))
FIRST = (((0,), (0,)), ((), ()))
PLAIN = (((1,), (0,)), ((), ()))


def dot(a, b, dims):
    return lax.dot_general(a, b, dims, preferred_element_type=jnp.float32)


def to_partner(block):
    count = lax.axis_size("lon")
    return lax.ppermute(block, "lon", [(i, i ^ 1) for i in range(count)])


def to_far(block, outward):
    count = lax.axis_size("lon")
    route = []
    for i in range(count):
        step = 2 if (i % 2 == 0) == outward else -2
        route.append((i, (i + step) % count))
    return lax.ppermute(block, "lon", route)


def to_twin(block):
    return lax.ppermute(block, "tm", [(0, 1), (1, 0)])


class Order:
    def __init__(self):
        self.token = jnp.zeros((), jnp.float32)

    def gate(self, value):
        return lax.optimization_barrier((self.token, value))[1]

    def passed(self, *values):
        self.token, *values = lax.optimization_barrier((self.token, *values))
        return values if len(values) > 1 else values[0]


def attention_kernel(
    bias_ref,
    own_q,
    par_q,
    own_a,
    own_b,
    par_a,
    par_b,
    yown_a,
    yown_b,
    rel_a,
    rel_b,
    own_out,
    par_out,
    near_own,
    near_par,
    near_far,
    near_rel,
    twin_stay,
    twin_send,
    scores_ref,
    probs_ref,
    dprobs_ref,
    grad_ref,
):
    rows = own_q.shape[2]
    lon = bias_ref.shape[2]
    scale = 1.0 / math.sqrt(HD)
    factor = math.log2(math.e) * scale
    ring = (rel_a, rel_b, own_a, own_b, par_a, par_b, yown_a, yown_b)
    span = 6
    sides = ((own_q, own_out), (par_q, par_out))
    peaks, totals, outs, deltas, query_grads, parts = ([None, None] for _ in range(6))

    def score_step(which, at):
        score = dot(ring[2 * which + at][0, 0], sides[which][0][0, 0], LAST)
        score = score.reshape(rows // lon, lon, rows) + bias_ref[which, at // 2][None]
        scores_ref[which, at] = score.reshape(rows, rows)
        top = jnp.max(score, axis=0)
        peaks[which] = top if at == 0 else jnp.maximum(peaks[which], top)

    def peak_done(which):
        peaks[which] = jnp.max(peaks[which], axis=0, keepdims=True)
        totals[which] = jnp.zeros((lon, rows), jnp.float32)
        outs[which] = jnp.zeros((HD, rows), jnp.float32)

    def probs_step(which, at):
        expo = jnp.exp2((scores_ref[which, at] - peaks[which]) * factor)
        totals[which] += jnp.sum(expo.reshape(rows // lon, lon, rows), axis=0)
        probs = expo.astype(jnp.bfloat16)
        probs_ref[which, at] = probs
        value = ring[2 * which + at][0, 1]
        outs[which] += dot(value, probs, FIRST)
        dprobs_ref[which, at] = dot(value, sides[which][0][0, 1], LAST)

    def probs_done(which):
        query, grad = sides[which][0][0, 0], sides[which][0][0, 1]
        inverse = 1.0 / jnp.sum(totals[which], axis=0, keepdims=True)
        totals[which] = inverse
        column = jnp.broadcast_to(inverse, (HD, rows)).T
        parts[which] = (
            (query.astype(jnp.float32) * (column * scale)).astype(jnp.bfloat16),
            (grad.astype(jnp.float32) * column).astype(jnp.bfloat16),
        )
        attended = (outs[which] * inverse).astype(jnp.bfloat16)
        sides[which][1][0, 0] = attended.T
        product = grad.T.astype(jnp.float32) * attended.astype(jnp.float32)
        deltas[which] = jnp.sum(product, axis=0, keepdims=True)
        query_grads[which] = jnp.zeros((HD, rows), jnp.float32)

    def grad_step(which, at):
        place = 2 * which + at
        probs = probs_ref[which, at]
        dscores = probs.astype(jnp.float32) * (dprobs_ref[which, at] - deltas[which])
        dscores = dscores.astype(jnp.bfloat16)
        query_grads[which] += dot(ring[place][0, 0], dscores, FIRST)
        key_part = dot(dscores, parts[which][0], PLAIN)
        value_part = dot(probs, parts[which][1], PLAIN)
        if which == 0 or at >= 4:
            grad_ref[place, 0] = key_part
            grad_ref[place, 1] = value_part
        else:
            grad_ref[place, 0] += key_part
            grad_ref[place, 1] += value_part

    def grad_done(which):
        sides[which][1][0, 1] = (query_grads[which] * (totals[which] * scale)).T.astype(jnp.bfloat16)

    for at in range(span):
        score_step(0, at)
    peak_done(0)
    for at in range(span):
        probs_step(0, at)
        score_step(1, at)
    probs_done(0)
    peak_done(1)
    for at in range(span):
        grad_step(0, at)
        probs_step(1, at)
    grad_done(0)
    probs_done(1)
    for at in range(span):
        grad_step(1, at)
    grad_done(1)
    for b, (at, near_ref) in enumerate(((2, near_own), (4, near_par), (6, near_far), (0, near_rel))):
        near_ref[0] = grad_ref[at].astype(jnp.bfloat16)
        twin_ref = twin_stay if b < 2 else twin_send
        twin_ref[b % 2, 0] = grad_ref[at + 1].astype(jnp.bfloat16)


def attention(bias, own_q, partner_q, blocks, low, skip, heads):
    rows = own_q.shape[2]
    here = pl.BlockSpec((1, 2, rows, HD), lambda h: (h + low, 0, 0, 0))
    there = pl.BlockSpec((1, 2, rows, HD), lambda h: (h + skip, 0, 0, 0))
    one = pl.BlockSpec((1, 2, rows, HD), lambda h: (h, 0, 0, 0))
    whole = pl.BlockSpec(bias.shape, lambda h: (0, 0, 0, 0))
    flat = [part for pair in blocks for part in pair]
    pairs = (heads, 2, rows, HD)
    spread = (2, heads, 2, rows, HD)
    per_head = pl.BlockSpec((2, 1, 2, rows, HD), lambda h: (0, h, 0, 0, 0))
    operands = [pltpu.with_memory_space_constraint(x, pltpu.HBM) for x in (own_q, partner_q, *flat[:-1])]
    operands.append(pltpu.with_memory_space_constraint(flat[-1], pltpu.VMEM))
    return pl.pallas_call(
        attention_kernel,
        grid=(heads,),
        in_specs=[whole, here, there, here, here, there, there, here, here, there, there],
        out_specs=[one] * 6 + [per_head] * 2,
        out_shape=[
            pltpu.HBM(shape, jnp.bfloat16) for shape in [pairs] * 6 + [spread] * 2
        ],
        scratch_shapes=[
            pltpu.VMEM((2, 6, rows, rows), jnp.float32),
            pltpu.VMEM((2, 6, rows, rows), jnp.bfloat16),
            pltpu.VMEM((2, 6, rows, rows), jnp.float32),
            pltpu.VMEM((8, 2, rows, HD), jnp.float32),
        ],
        compiler_params=pltpu.CompilerParams(vmem_limit_bytes=26 * 1024 * 1024),
        cost_estimate=pl.CostEstimate(
            flops=heads * 2 * 6 * 6 * 2 * rows * rows * HD, bytes_accessed=heads * 28 * rows * HD * 2, transcendentals=0
        ),
        name="attention",
    )(bias, *operands)


def window_bias(offsets, side, frames, lats, lons):
    lat_tiles, lon_tiles = offsets.shape[1:]
    per_row = jnp.repeat(jnp.repeat(offsets, TILE, axis=1), TILE, axis=2)
    centre = per_row + (jnp.arange(lons) // TILE)[None, None, :]
    centre = jnp.broadcast_to(centre[:, None], (2, frames, lats, lons)).reshape(2, -1)
    sign = 1 - 2 * side
    place = jnp.arange(lons) // TILE
    shift = jnp.array([[-1, 0, 1], [-1, 0, 1]], jnp.int32) * sign * lon_tiles
    column = shift[:, :, None] + place[None, None, :]
    near = jnp.abs(column[:, :, :, None] - centre[:, None, None, :]) <= 1
    return jnp.where(near, 0.0, MASKED).astype(jnp.float32)


def on_device(query_rows, key_rows, value_rows, out_grad, window_offsets):
    frames, lats, lons, width = query_rows.shape
    heads = width // HD
    half = heads // 2
    rows = frames * lats * lons
    frame_tiles = frames // TILE * lax.axis_size("tm")
    if lax.axis_size("tm") != 2 or frame_tiles > 2 or lats // TILE > 2 or lons != 2 * TILE or heads % 2:
        raise ValueError("unsupported block")
    side = lax.axis_index("lon") % 2

    def by_head(*arrays):
        pair = jnp.stack(arrays).reshape(len(arrays), frames, lats, lons, heads, HD)
        return pair.transpose(4, 0, 1, 2, 3, 5).reshape(heads, len(arrays), rows, HD)

    def half_of(array, which):
        return lax.dynamic_slice_in_dim(array, which * half, half, 0)

    key_value = by_head(key_rows, value_rows)
    mine_kv, theirs_kv = half_of(key_value, side), half_of(key_value, 1 - side)
    query_grad = by_head(query_rows, out_grad)
    mine_qg, theirs_qg = half_of(query_grad, side), half_of(query_grad, 1 - side)
    offsets = window_offsets.reshape(lats // TILE, lons // TILE)

    first = min(FIRST_HEADS, half - 1)
    last = half - min(LAST_HEADS, half - first)
    order = Order()
    far = to_far(mine_kv, False)
    partner_0 = to_partner(theirs_kv[:first])
    both = to_partner(order.gate(offsets))
    partner_1 = to_partner(theirs_kv[first:])
    own_b = to_twin(mine_kv)
    partner_0 = order.passed(partner_0)
    relay_0 = to_far(order.gate(partner_0), True)
    part_q0 = to_partner(order.gate(theirs_qg[:first]))
    relay_0, part_q0, far, partner_1, both, own_b = order.passed(relay_0, part_q0, far, partner_1, both, own_b)
    bias = window_bias(jnp.stack([offsets, both]), side, frames, lats, lons)
    relay_0b = to_twin(order.gate(relay_0))
    far_b = to_twin(order.gate(far))
    partner_0b = to_twin(order.gate(partner_0))
    relay_1 = to_far(order.gate(partner_1), True)
    part_q1 = to_partner(order.gate(theirs_qg[first:]))
    relay_0b, partner_0b, far_b = order.passed(relay_0b, partner_0b, far_b)
    partner_1b = to_twin(order.gate(partner_1))

    def compute(low, high, partner, relay, part_q):
        skip = low - (first if low else 0)
        blocks = [(mine_kv, own_b), partner, (far, far_b), relay]
        return attention(order.gate(bias), mine_qg, part_q, blocks, low, skip, high - low)

    def total(near, twin, block):
        return near[block] + twin[block % 2].astype(jnp.float32)

    def rounded(near, twin, block):
        return total(near, twin, block).astype(jnp.bfloat16)

    def theirs_total(near, twin, back):
        return (total(near, twin, 1) + back.astype(jnp.float32)).astype(jnp.bfloat16)

    done_0, out_0, *near_0, stay_0, send_0 = compute(
        0, first, (partner_0, partner_0b), (relay_0, relay_0b), part_q0
    )
    send_0, relay_1, part_q1, partner_1b = order.passed(send_0, relay_1, part_q1, partner_1b)
    send_0 = to_twin(order.gate(send_0))
    relay_1b = to_twin(order.gate(relay_1))
    send_0, relay_1b = order.passed(send_0, relay_1b)
    back_0 = to_far(rounded(near_0, send_0, 3), False)
    back_out_0 = to_partner(order.gate(out_0))
    stay_0 = to_twin(order.gate(stay_0))

    rest = (partner_1, partner_1b), (relay_1, relay_1b), part_q1
    done_1, out_1, *near_1, stay_1, send_1 = compute(first, last, *rest)
    send_1, back_0, back_out_0, stay_0 = order.passed(send_1, back_0, back_out_0, stay_0)
    send_1 = to_twin(order.gate(send_1))
    theirs_0 = theirs_total(near_0, stay_0, order.gate(back_0))
    mixed_1 = to_partner(jnp.concatenate([theirs_0, order.gate(out_1)]))
    send_1 = order.passed(send_1)
    back_1 = to_far(rounded(near_1, send_1, 3), False)
    ahead_0 = to_far(order.gate(rounded(near_0, send_0, 2)), True)
    stay_1 = to_twin(order.gate(stay_1))

    done_2, out_2, *near_2, stay_2, send_2 = compute(last, half, *rest)
    send_2, back_1, stay_1, mixed_1 = order.passed(send_2, back_1, stay_1, mixed_1)
    send_2 = to_twin(order.gate(send_2))
    theirs_1 = theirs_total(near_1, stay_1, order.gate(back_1))
    payload = jnp.concatenate([theirs_1, order.gate(out_2)])
    send_2 = order.passed(send_2)
    outward = rounded(near_2, send_2, 3)
    outward, payload, ahead_0 = order.passed(outward, payload, ahead_0)
    back_2 = to_far(outward, False)
    mixed_2 = to_partner(payload)
    stay_2 = to_twin(order.gate(stay_2))
    back_2, stay_2 = order.passed(back_2, stay_2)
    theirs_2 = to_partner(theirs_total(near_2, stay_2, order.gate(back_2)))
    ahead_12 = to_far(order.gate(jnp.concatenate([rounded(near_1, send_1, 2), rounded(near_2, send_2, 2)])), True)

    theirs_0, back_out_1 = mixed_1[:first], mixed_1[first:]
    theirs_1, back_out_2 = mixed_2[: last - first], mixed_2[last - first :]
    def assembled(mine, theirs):
        mine, theirs = jnp.concatenate(mine), jnp.concatenate(theirs)
        low = jnp.where(side == 0, mine, theirs)
        high = jnp.where(side == 0, theirs, mine)
        array = jnp.concatenate([low, high])
        shaped = array.reshape(heads, 2, frames, lats, lons, HD).transpose(1, 2, 3, 4, 0, 5)
        shaped = shaped.reshape(2, frames, lats, lons, width)
        return shaped[0], shaped[1]

    attended, query_out = assembled((done_0, done_1, done_2), (back_out_0, back_out_1, back_out_2))
    theirs_2, ahead_12, attended, query_out = order.passed(theirs_2, ahead_12, attended, query_out)
    ahead_1, ahead_2 = ahead_12[: last - first], ahead_12[last - first :]
    mine = [
        (total(near, twin, 0) + ahead.astype(jnp.float32)).astype(jnp.bfloat16)
        for near, twin, ahead in ((near_0, stay_0, ahead_0), (near_1, stay_1, ahead_1), (near_2, stay_2, ahead_2))
    ]
    key_out, value_out = assembled(mine, (theirs_0, theirs_1, theirs_2))
    return attended, query_out, key_out, value_out


def solution(mesh):
    rows = P("tm", None, "lon", "head")
    return jax.shard_map(
        on_device,
        mesh=mesh,
        in_specs=(rows, rows, rows, rows, P("tm", None, "lon")),
        out_specs=(rows, rows, rows, rows),
        check_vma=False,
    )
```

```python
import math

import jax
import jax.numpy as jnp
from jax import lax
from jax.experimental import pallas as pl
from jax.experimental.pallas import tpu as pltpu
from jax.sharding import PartitionSpec as P

HD = 128
TILE = 4
MASKED = -1e30
FIRST_HEADS = 2
LAST_HEADS = 1

LAST = (((1,), (1,)), ((), ()))
FIRST = (((0,), (0,)), ((), ()))
PLAIN = (((1,), (0,)), ((), ()))


def dot(a, b, dims):
    return lax.dot_general(a, b, dims, preferred_element_type=jnp.float32)


def to_partner(block):
    count = lax.axis_size("lon")
    return lax.ppermute(block, "lon", [(i, i ^ 1) for i in range(count)])


def to_far(block, outward):
    count = lax.axis_size("lon")
    route = []
    for i in range(count):
        step = 2 if (i % 2 == 0) == outward else -2
        route.append((i, (i + step) % count))
    return lax.ppermute(block, "lon", route)


def to_twin(block):
    return lax.ppermute(block, "tm", [(0, 1), (1, 0)])


class Order:
    def __init__(self):
        self.token = jnp.zeros((), jnp.float32)

    def gate(self, value):
        return lax.optimization_barrier((self.token, value))[1]

    def passed(self, *values):
        self.token, *values = lax.optimization_barrier((self.token, *values))
        return values if len(values) > 1 else values[0]


def attention_kernel(
    bias_ref,
    own_q,
    par_q,
    own_a,
    own_b,
    par_a,
    par_b,
    yown_a,
    yown_b,
    rel_a,
    rel_b,
    own_out,
    par_out,
    near_own,
    near_par,
    near_far,
    near_rel,
    twin_stay,
    twin_send,
    scores_ref,
    probs_ref,
    dprobs_ref,
    grad_ref,
):
    rows = own_q.shape[2]
    lon = bias_ref.shape[2]
    scale = 1.0 / math.sqrt(HD)
    factor = math.log2(math.e) * scale
    ring = (rel_a, rel_b, own_a, own_b, par_a, par_b, yown_a, yown_b)
    span = 6
    sides = ((own_q, own_out), (par_q, par_out))
    peaks, totals, outs, deltas, query_grads, parts = ([None, None] for _ in range(6))

    def score_step(which, at):
        score = dot(ring[2 * which + at][0, 0], sides[which][0][0, 0], LAST)
        score = score.reshape(rows // lon, lon, rows) + bias_ref[which, at // 2][None]
        scores_ref[which, at] = score.reshape(rows, rows)
        top = jnp.max(score, axis=0)
        peaks[which] = top if at == 0 else jnp.maximum(peaks[which], top)

    def peak_done(which):
        peaks[which] = jnp.max(peaks[which], axis=0, keepdims=True)
        totals[which] = jnp.zeros((lon, rows), jnp.float32)
        outs[which] = jnp.zeros((HD, rows), jnp.float32)

    def probs_step(which, at):
        expo = jnp.exp2((scores_ref[which, at] - peaks[which]) * factor)
        totals[which] += jnp.sum(expo.reshape(rows // lon, lon, rows), axis=0)
        probs = expo.astype(jnp.bfloat16)
        probs_ref[which, at] = probs
        value = ring[2 * which + at][0, 1]
        outs[which] += dot(value, probs, FIRST)
        dprobs_ref[which, at] = dot(value, sides[which][0][0, 1], LAST)

    def probs_done(which):
        query, grad = sides[which][0][0, 0], sides[which][0][0, 1]
        inverse = 1.0 / jnp.sum(totals[which], axis=0, keepdims=True)
        totals[which] = inverse
        column = jnp.broadcast_to(inverse, (HD, rows)).T
        parts[which] = (
            (query.astype(jnp.float32) * (column * scale)).astype(jnp.bfloat16),
            (grad.astype(jnp.float32) * column).astype(jnp.bfloat16),
        )
        attended = (outs[which] * inverse).astype(jnp.bfloat16)
        sides[which][1][0, 0] = attended.T
        product = grad.T.astype(jnp.float32) * attended.astype(jnp.float32)
        deltas[which] = jnp.sum(product, axis=0, keepdims=True)
        query_grads[which] = jnp.zeros((HD, rows), jnp.float32)

    def grad_step(which, at):
        place = 2 * which + at
        probs = probs_ref[which, at]
        dscores = probs.astype(jnp.float32) * (dprobs_ref[which, at] - deltas[which])
        dscores = dscores.astype(jnp.bfloat16)
        query_grads[which] += dot(ring[place][0, 0], dscores, FIRST)
        key_part = dot(dscores, parts[which][0], PLAIN)
        value_part = dot(probs, parts[which][1], PLAIN)
        if which == 0 or at >= 4:
            grad_ref[place, 0] = key_part
            grad_ref[place, 1] = value_part
        else:
            grad_ref[place, 0] += key_part
            grad_ref[place, 1] += value_part

    def grad_done(which):
        sides[which][1][0, 1] = (query_grads[which] * (totals[which] * scale)).T.astype(jnp.bfloat16)

    for at in range(span):
        score_step(0, at)
    peak_done(0)
    for at in range(span):
        probs_step(0, at)
        score_step(1, at)
    probs_done(0)
    peak_done(1)
    for at in range(span):
        grad_step(0, at)
        probs_step(1, at)
    grad_done(0)
    probs_done(1)
    for at in range(span):
        grad_step(1, at)
    grad_done(1)
    for b, (at, near_ref) in enumerate(((2, near_own), (4, near_par), (6, near_far), (0, near_rel))):
        near_ref[0] = grad_ref[at].astype(jnp.bfloat16)
        twin_ref = twin_stay if b < 2 else twin_send
        twin_ref[b % 2, 0] = grad_ref[at + 1].astype(jnp.bfloat16)


def attention(bias, own_q, partner_q, blocks, low, skip, heads):
    rows = own_q.shape[2]
    here = pl.BlockSpec((1, 2, rows, HD), lambda h: (h + low, 0, 0, 0))
    there = pl.BlockSpec((1, 2, rows, HD), lambda h: (h + skip, 0, 0, 0))
    one = pl.BlockSpec((1, 2, rows, HD), lambda h: (h, 0, 0, 0))
    whole = pl.BlockSpec(bias.shape, lambda h: (0, 0, 0, 0))
    flat = [part for pair in blocks for part in pair]
    pairs = (heads, 2, rows, HD)
    spread = (2, heads, 2, rows, HD)
    per_head = pl.BlockSpec((2, 1, 2, rows, HD), lambda h: (0, h, 0, 0, 0))
    operands = [pltpu.with_memory_space_constraint(x, pltpu.HBM) for x in (own_q, partner_q, *flat[:-1])]
    operands.append(pltpu.with_memory_space_constraint(flat[-1], pltpu.VMEM))
    return pl.pallas_call(
        attention_kernel,
        grid=(heads,),
        in_specs=[whole, here, there, here, here, there, there, here, here, there, there],
        out_specs=[one] * 6 + [per_head] * 2,
        out_shape=[
            jax.ShapeDtypeStruct(shape, jnp.bfloat16) for shape in [pairs] * 6 + [spread] * 2
        ],
        scratch_shapes=[
            pltpu.VMEM((2, 6, rows, rows), jnp.float32),
            pltpu.VMEM((2, 6, rows, rows), jnp.bfloat16),
            pltpu.VMEM((2, 6, rows, rows), jnp.float32),
            pltpu.VMEM((8, 2, rows, HD), jnp.float32),
        ],
        compiler_params=pltpu.CompilerParams(vmem_limit_bytes=26 * 1024 * 1024),
        cost_estimate=pl.CostEstimate(
            flops=heads * 2 * 6 * 6 * 2 * rows * rows * HD, bytes_accessed=heads * 28 * rows * HD * 2, transcendentals=0
        ),
        name="attention",
    )(bias, *operands)


def window_bias(offsets, side, frames, lats, lons):
    lat_tiles, lon_tiles = offsets.shape[1:]
    per_row = jnp.repeat(jnp.repeat(offsets, TILE, axis=1), TILE, axis=2)
    centre = per_row + (jnp.arange(lons) // TILE)[None, None, :]
    centre = jnp.broadcast_to(centre[:, None], (2, frames, lats, lons)).reshape(2, -1)
    sign = 1 - 2 * side
    place = jnp.arange(lons) // TILE
    shift = jnp.array([[-1, 0, 1], [-1, 0, 1]], jnp.int32) * sign * lon_tiles
    column = shift[:, :, None] + place[None, None, :]
    near = jnp.abs(column[:, :, :, None] - centre[:, None, None, :]) <= 1
    return jnp.where(near, 0.0, MASKED).astype(jnp.float32)


def on_device(query_rows, key_rows, value_rows, out_grad, window_offsets):
    frames, lats, lons, width = query_rows.shape
    heads = width // HD
    half = heads // 2
    rows = frames * lats * lons
    frame_tiles = frames // TILE * lax.axis_size("tm")
    if lax.axis_size("tm") != 2 or frame_tiles > 2 or lats // TILE > 2 or lons != 2 * TILE or heads % 2:
        raise ValueError("unsupported block")
    side = lax.axis_index("lon") % 2

    def by_head(*arrays):
        pair = jnp.stack(arrays).reshape(len(arrays), frames, lats, lons, heads, HD)
        return pair.transpose(4, 0, 1, 2, 3, 5).reshape(heads, len(arrays), rows, HD)

    def half_of(array, which):
        return lax.dynamic_slice_in_dim(array, which * half, half, 0)

    key_value = by_head(key_rows, value_rows)
    mine_kv, theirs_kv = half_of(key_value, side), half_of(key_value, 1 - side)
    query_grad = by_head(query_rows, out_grad)
    mine_qg, theirs_qg = half_of(query_grad, side), half_of(query_grad, 1 - side)
    offsets = window_offsets.reshape(lats // TILE, lons // TILE)

    first = min(FIRST_HEADS, half - 1)
    last = half - min(LAST_HEADS, half - first)
    order = Order()
    far = to_far(mine_kv, False)
    partner_0 = to_partner(theirs_kv[:first])
    both = to_partner(order.gate(offsets))
    partner_1 = to_partner(theirs_kv[first:])
    own_b = to_twin(mine_kv)
    partner_0 = order.passed(partner_0)
    relay_0 = to_far(order.gate(partner_0), True)
    part_q0 = to_partner(order.gate(theirs_qg[:first]))
    relay_0, part_q0, far, partner_1, both, own_b = order.passed(relay_0, part_q0, far, partner_1, both, own_b)
    bias = window_bias(jnp.stack([offsets, both]), side, frames, lats, lons)
    relay_0b = to_twin(order.gate(relay_0))
    far_b = to_twin(order.gate(far))
    partner_0b = to_twin(order.gate(partner_0))
    relay_1 = to_far(order.gate(partner_1), True)
    part_q1 = to_partner(order.gate(theirs_qg[first:]))
    relay_0b, partner_0b, far_b = order.passed(relay_0b, partner_0b, far_b)
    partner_1b = to_twin(order.gate(partner_1))

    def compute(low, high, partner, relay, part_q):
        skip = low - (first if low else 0)
        blocks = [(mine_kv, own_b), partner, (far, far_b), relay]
        return attention(order.gate(bias), mine_qg, part_q, blocks, low, skip, high - low)

    def total(near, twin, block):
        return near[block] + twin[block % 2].astype(jnp.float32)

    def rounded(near, twin, block):
        return total(near, twin, block).astype(jnp.bfloat16)

    def theirs_total(near, twin, back):
        return (total(near, twin, 1) + back.astype(jnp.float32)).astype(jnp.bfloat16)

    done_0, out_0, *near_0, stay_0, send_0 = compute(
        0, first, (partner_0, partner_0b), (relay_0, relay_0b), part_q0
    )
    send_0, relay_1, part_q1, partner_1b = order.passed(send_0, relay_1, part_q1, partner_1b)
    send_0 = to_twin(order.gate(send_0))
    relay_1b = to_twin(order.gate(relay_1))
    send_0, relay_1b = order.passed(send_0, relay_1b)
    back_0 = to_far(rounded(near_0, send_0, 3), False)
    back_out_0 = to_partner(order.gate(out_0))
    stay_0 = to_twin(order.gate(stay_0))

    rest = (partner_1, partner_1b), (relay_1, relay_1b), part_q1
    done_1, out_1, *near_1, stay_1, send_1 = compute(first, last, *rest)
    send_1, back_0, back_out_0, stay_0 = order.passed(send_1, back_0, back_out_0, stay_0)
    send_1 = to_twin(order.gate(send_1))
    theirs_0 = theirs_total(near_0, stay_0, order.gate(back_0))
    mixed_1 = to_partner(jnp.concatenate([theirs_0, order.gate(out_1)]))
    send_1 = order.passed(send_1)
    back_1 = to_far(rounded(near_1, send_1, 3), False)
    ahead_0 = to_far(order.gate(rounded(near_0, send_0, 2)), True)
    stay_1 = to_twin(order.gate(stay_1))

    done_2, out_2, *near_2, stay_2, send_2 = compute(last, half, *rest)
    send_2, back_1, stay_1, mixed_1 = order.passed(send_2, back_1, stay_1, mixed_1)
    send_2 = to_twin(order.gate(send_2))
    theirs_1 = theirs_total(near_1, stay_1, order.gate(back_1))
    payload = jnp.concatenate([theirs_1, order.gate(out_2)])
    send_2 = order.passed(send_2)
    outward = rounded(near_2, send_2, 3)
    outward, payload, ahead_0 = order.passed(outward, payload, ahead_0)
    back_2 = to_far(outward, False)
    mixed_2 = to_partner(payload)
    stay_2 = to_twin(order.gate(stay_2))
    back_2, stay_2 = order.passed(back_2, stay_2)
    theirs_2 = to_partner(theirs_total(near_2, stay_2, order.gate(back_2)))
    ahead_12 = to_far(order.gate(jnp.concatenate([rounded(near_1, send_1, 2), rounded(near_2, send_2, 2)])), True)

    theirs_0, back_out_1 = mixed_1[:first], mixed_1[first:]
    theirs_1, back_out_2 = mixed_2[: last - first], mixed_2[last - first :]
    def assembled(mine, theirs):
        mine, theirs = jnp.concatenate(mine), jnp.concatenate(theirs)
        low = jnp.where(side == 0, mine, theirs)
        high = jnp.where(side == 0, theirs, mine)
        array = jnp.concatenate([low, high])
        shaped = array.reshape(heads, 2, frames, lats, lons, HD).transpose(1, 2, 3, 4, 0, 5)
        shaped = shaped.reshape(2, frames, lats, lons, width)
        return shaped[0], shaped[1]

    attended, query_out = assembled((done_0, done_1, done_2), (back_out_0, back_out_1, back_out_2))
    theirs_2, ahead_12, attended, query_out = order.passed(theirs_2, ahead_12, attended, query_out)
    ahead_1, ahead_2 = ahead_12[: last - first], ahead_12[last - first :]
    mine = [
        (total(near, twin, 0) + ahead.astype(jnp.float32)).astype(jnp.bfloat16)
        for near, twin, ahead in ((near_0, stay_0, ahead_0), (near_1, stay_1, ahead_1), (near_2, stay_2, ahead_2))
    ]
    key_out, value_out = assembled(mine, (theirs_0, theirs_1, theirs_2))
    return attended, query_out, key_out, value_out


def solution(mesh):
    rows = P("tm", None, "lon", "head")
    return jax.shard_map(
        on_device,
        mesh=mesh,
        in_specs=(rows, rows, rows, rows, P("tm", None, "lon")),
        out_specs=(rows, rows, rows, rows),
        check_vma=False,
    )
```

```python
import math

import jax
import jax.numpy as jnp
from jax import lax
from jax.experimental import pallas as pl
from jax.experimental.pallas import tpu as pltpu
from jax.sharding import PartitionSpec as P

HD = 128
TILE = 4
MASKED = -1e30
FIRST_HEADS = 2
LAST_HEADS = 1

LAST = (((1,), (1,)), ((), ()))
FIRST = (((0,), (0,)), ((), ()))
PLAIN = (((1,), (0,)), ((), ()))


def dot(a, b, dims):
    return lax.dot_general(a, b, dims, preferred_element_type=jnp.float32)


def to_partner(block):
    count = lax.axis_size("lon")
    return lax.ppermute(block, "lon", [(i, i ^ 1) for i in range(count)])


def to_far(block, outward):
    count = lax.axis_size("lon")
    route = []
    for i in range(count):
        step = 2 if (i % 2 == 0) == outward else -2
        route.append((i, (i + step) % count))
    return lax.ppermute(block, "lon", route)


def to_twin(block):
    return lax.ppermute(block, "tm", [(0, 1), (1, 0)])


class Order:
    def __init__(self):
        self.token = jnp.zeros((), jnp.float32)

    def gate(self, value):
        return lax.optimization_barrier((self.token, value))[1]

    def passed(self, *values):
        self.token, *values = lax.optimization_barrier((self.token, *values))
        return values if len(values) > 1 else values[0]


def attention_kernel(
    bias_ref,
    own_q,
    par_q,
    own_a,
    own_b,
    par_a,
    par_b,
    yown_a,
    yown_b,
    rel_a,
    rel_b,
    own_out,
    par_out,
    near_own,
    near_par,
    near_far,
    near_rel,
    twin_stay,
    twin_send,
    scores_ref,
    probs_ref,
    dprobs_ref,
    grad_ref,
):
    rows = own_q.shape[2]
    lon = bias_ref.shape[2]
    scale = 1.0 / math.sqrt(HD)
    factor = math.log2(math.e) * scale
    ring = (rel_a, rel_b, own_a, own_b, par_a, par_b, yown_a, yown_b)
    span = 6
    sides = ((own_q, own_out), (par_q, par_out))
    peaks, totals, outs, deltas, query_grads, parts = ([None, None] for _ in range(6))

    def score_step(which, at):
        score = dot(ring[2 * which + at][0, 0], sides[which][0][0, 0], LAST)
        score = score.reshape(rows // lon, lon, rows) + bias_ref[which, at // 2][None]
        scores_ref[which, at] = score.reshape(rows, rows)
        top = jnp.max(score, axis=0)
        peaks[which] = top if at == 0 else jnp.maximum(peaks[which], top)

    def peak_done(which):
        peaks[which] = jnp.max(peaks[which], axis=0, keepdims=True)
        totals[which] = jnp.zeros((lon, rows), jnp.float32)
        outs[which] = jnp.zeros((HD, rows), jnp.float32)

    def probs_step(which, at):
        expo = jnp.exp2((scores_ref[which, at] - peaks[which]) * factor)
        totals[which] += jnp.sum(expo.reshape(rows // lon, lon, rows), axis=0)
        probs = expo.astype(jnp.bfloat16)
        probs_ref[which, at] = probs
        value = ring[2 * which + at][0, 1]
        outs[which] += dot(value, probs, FIRST)
        dprobs_ref[which, at] = dot(value, sides[which][0][0, 1], LAST)

    def probs_done(which):
        query, grad = sides[which][0][0, 0], sides[which][0][0, 1]
        inverse = 1.0 / jnp.sum(totals[which], axis=0, keepdims=True)
        totals[which] = inverse
        column = jnp.broadcast_to(inverse, (HD, rows)).T
        parts[which] = (
            (query.astype(jnp.float32) * (column * scale)).astype(jnp.bfloat16),
            (grad.astype(jnp.float32) * column).astype(jnp.bfloat16),
        )
        attended = (outs[which] * inverse).astype(jnp.bfloat16)
        sides[which][1][0, 0] = attended.T
        product = grad.T.astype(jnp.float32) * attended.astype(jnp.float32)
        deltas[which] = jnp.sum(product, axis=0, keepdims=True)
        query_grads[which] = jnp.zeros((HD, rows), jnp.float32)

    def grad_step(which, at):
        place = 2 * which + at
        probs = probs_ref[which, at]
        dscores = probs.astype(jnp.float32) * (dprobs_ref[which, at] - deltas[which])
        dscores = dscores.astype(jnp.bfloat16)
        query_grads[which] += dot(ring[place][0, 0], dscores, FIRST)
        key_part = dot(dscores, parts[which][0], PLAIN)
        value_part = dot(probs, parts[which][1], PLAIN)
        if which == 0 or at >= 4:
            grad_ref[place, 0] = key_part
            grad_ref[place, 1] = value_part
        else:
            grad_ref[place, 0] += key_part
            grad_ref[place, 1] += value_part

    def grad_done(which):
        sides[which][1][0, 1] = (query_grads[which] * (totals[which] * scale)).T.astype(jnp.bfloat16)

    for at in range(span):
        score_step(0, at)
    peak_done(0)
    for at in range(span):
        probs_step(0, at)
        score_step(1, at)
    probs_done(0)
    peak_done(1)
    for at in range(span):
        grad_step(0, at)
        probs_step(1, at)
    grad_done(0)
    probs_done(1)
    for at in range(span):
        grad_step(1, at)
    grad_done(1)
    for b, (at, near_ref) in enumerate(((2, near_own), (4, near_par), (6, near_far), (0, near_rel))):
        near_ref[0] = grad_ref[at].astype(jnp.bfloat16)
        twin_ref = twin_stay if b < 2 else twin_send
        twin_ref[b % 2, 0] = grad_ref[at + 1].astype(jnp.bfloat16)


def attention(bias, own_q, partner_q, blocks, low, skip, heads):
    rows = own_q.shape[2]
    here = pl.BlockSpec((1, 2, rows, HD), lambda h: (h + low, 0, 0, 0))
    there = pl.BlockSpec((1, 2, rows, HD), lambda h: (h + skip, 0, 0, 0))
    one = pl.BlockSpec((1, 2, rows, HD), lambda h: (h, 0, 0, 0))
    whole = pl.BlockSpec(bias.shape, lambda h: (0, 0, 0, 0))
    flat = [part for pair in blocks for part in pair]
    pairs = (heads, 2, rows, HD)
    spread = (2, heads, 2, rows, HD)
    per_head = pl.BlockSpec((2, 1, 2, rows, HD), lambda h: (0, h, 0, 0, 0))
    operands = [pltpu.with_memory_space_constraint(x, pltpu.HBM) for x in (own_q, partner_q, *flat[:-1])]
    operands.append(pltpu.with_memory_space_constraint(flat[-1], pltpu.VMEM))
    return pl.pallas_call(
        attention_kernel,
        grid=(heads,),
        in_specs=[whole, here, there, here, here, there, there, here, here, there, there],
        out_specs=[one] * 6 + [per_head] * 2,
        out_shape=[
            jax.ShapeDtypeStruct(shape, jnp.bfloat16) for shape in [pairs] * 6 + [spread] * 2
        ],
        scratch_shapes=[
            pltpu.VMEM((2, 6, rows, rows), jnp.float32),
            pltpu.VMEM((2, 6, rows, rows), jnp.bfloat16),
            pltpu.VMEM((2, 6, rows, rows), jnp.float32),
            pltpu.VMEM((8, 2, rows, HD), jnp.float32),
        ],
        compiler_params=pltpu.CompilerParams(vmem_limit_bytes=20 * 1024 * 1024),
        cost_estimate=pl.CostEstimate(
            flops=heads * 2 * 6 * 6 * 2 * rows * rows * HD, bytes_accessed=heads * 28 * rows * HD * 2, transcendentals=0
        ),
        name="attention",
    )(bias, *operands)


def window_bias(offsets, side, frames, lats, lons):
    lat_tiles, lon_tiles = offsets.shape[1:]
    per_row = jnp.repeat(jnp.repeat(offsets, TILE, axis=1), TILE, axis=2)
    centre = per_row + (jnp.arange(lons) // TILE)[None, None, :]
    centre = jnp.broadcast_to(centre[:, None], (2, frames, lats, lons)).reshape(2, -1)
    sign = 1 - 2 * side
    place = jnp.arange(lons) // TILE
    shift = jnp.array([[-1, 0, 1], [-1, 0, 1]], jnp.int32) * sign * lon_tiles
    column = shift[:, :, None] + place[None, None, :]
    near = jnp.abs(column[:, :, :, None] - centre[:, None, None, :]) <= 1
    return jnp.where(near, 0.0, MASKED).astype(jnp.float32)


def on_device(query_rows, key_rows, value_rows, out_grad, window_offsets):
    frames, lats, lons, width = query_rows.shape
    heads = width // HD
    half = heads // 2
    rows = frames * lats * lons
    frame_tiles = frames // TILE * lax.axis_size("tm")
    if lax.axis_size("tm") != 2 or frame_tiles > 2 or lats // TILE > 2 or lons != 2 * TILE or heads % 2:
        raise ValueError("unsupported block")
    side = lax.axis_index("lon") % 2

    def by_head(*arrays):
        pair = jnp.stack(arrays).reshape(len(arrays), frames, lats, lons, heads, HD)
        return pair.transpose(4, 0, 1, 2, 3, 5).reshape(heads, len(arrays), rows, HD)

    def half_of(array, which):
        return lax.dynamic_slice_in_dim(array, which * half, half, 0)

    key_value = by_head(key_rows, value_rows)
    mine_kv, theirs_kv = half_of(key_value, side), half_of(key_value, 1 - side)
    query_grad = by_head(query_rows, out_grad)
    mine_qg, theirs_qg = half_of(query_grad, side), half_of(query_grad, 1 - side)
    offsets = window_offsets.reshape(lats // TILE, lons // TILE)

    first = min(FIRST_HEADS, half - 1)
    last = half - min(LAST_HEADS, half - first)
    order = Order()
    far = to_far(mine_kv, False)
    partner_0 = to_partner(theirs_kv[:first])
    both = to_partner(order.gate(offsets))
    partner_1 = to_partner(theirs_kv[first:])
    own_b = to_twin(mine_kv)
    partner_0 = order.passed(partner_0)
    relay_0 = to_far(order.gate(partner_0), True)
    part_q0 = to_partner(order.gate(theirs_qg[:first]))
    relay_0, part_q0, far, partner_1, both, own_b = order.passed(relay_0, part_q0, far, partner_1, both, own_b)
    bias = window_bias(jnp.stack([offsets, both]), side, frames, lats, lons)
    relay_0b = to_twin(order.gate(relay_0))
    far_b = to_twin(order.gate(far))
    partner_0b = to_twin(order.gate(partner_0))
    relay_1 = to_far(order.gate(partner_1), True)
    part_q1 = to_partner(order.gate(theirs_qg[first:]))
    relay_0b, partner_0b, far_b = order.passed(relay_0b, partner_0b, far_b)
    partner_1b = to_twin(order.gate(partner_1))

    def compute(low, high, partner, relay, part_q):
        skip = low - (first if low else 0)
        blocks = [(mine_kv, own_b), partner, (far, far_b), relay]
        return attention(order.gate(bias), mine_qg, part_q, blocks, low, skip, high - low)

    def total(near, twin, block):
        return near[block] + twin[block % 2].astype(jnp.float32)

    def rounded(near, twin, block):
        return total(near, twin, block).astype(jnp.bfloat16)

    def theirs_total(near, twin, back):
        return (total(near, twin, 1) + back.astype(jnp.float32)).astype(jnp.bfloat16)

    done_0, out_0, *near_0, stay_0, send_0 = compute(
        0, first, (partner_0, partner_0b), (relay_0, relay_0b), part_q0
    )
    send_0, relay_1, part_q1, partner_1b = order.passed(send_0, relay_1, part_q1, partner_1b)
    send_0 = to_twin(order.gate(send_0))
    relay_1b = to_twin(order.gate(relay_1))
    send_0, relay_1b = order.passed(send_0, relay_1b)
    back_0 = to_far(rounded(near_0, send_0, 3), False)
    back_out_0 = to_partner(order.gate(out_0))
    stay_0 = to_twin(order.gate(stay_0))

    rest = (partner_1, partner_1b), (relay_1, relay_1b), part_q1
    done_1, out_1, *near_1, stay_1, send_1 = compute(first, last, *rest)
    send_1, back_0, back_out_0, stay_0 = order.passed(send_1, back_0, back_out_0, stay_0)
    send_1 = to_twin(order.gate(send_1))
    theirs_0 = theirs_total(near_0, stay_0, order.gate(back_0))
    mixed_1 = to_partner(jnp.concatenate([theirs_0, order.gate(out_1)]))
    send_1 = order.passed(send_1)
    back_1 = to_far(rounded(near_1, send_1, 3), False)
    ahead_0 = to_far(order.gate(rounded(near_0, send_0, 2)), True)
    stay_1 = to_twin(order.gate(stay_1))

    done_2, out_2, *near_2, stay_2, send_2 = compute(last, half, *rest)
    send_2, back_1, stay_1, mixed_1 = order.passed(send_2, back_1, stay_1, mixed_1)
    send_2 = to_twin(order.gate(send_2))
    theirs_1 = theirs_total(near_1, stay_1, order.gate(back_1))
    payload = jnp.concatenate([theirs_1, order.gate(out_2)])
    send_2 = order.passed(send_2)
    outward = rounded(near_2, send_2, 3)
    outward, payload, ahead_0 = order.passed(outward, payload, ahead_0)
    back_2 = to_far(outward, False)
    mixed_2 = to_partner(payload)
    stay_2 = to_twin(order.gate(stay_2))
    back_2, stay_2 = order.passed(back_2, stay_2)
    theirs_2 = to_partner(theirs_total(near_2, stay_2, order.gate(back_2)))
    ahead_12 = to_far(order.gate(jnp.concatenate([rounded(near_1, send_1, 2), rounded(near_2, send_2, 2)])), True)

    theirs_0, back_out_1 = mixed_1[:first], mixed_1[first:]
    theirs_1, back_out_2 = mixed_2[: last - first], mixed_2[last - first :]
    def assembled(mine, theirs):
        mine, theirs = jnp.concatenate(mine), jnp.concatenate(theirs)
        low = jnp.where(side == 0, mine, theirs)
        high = jnp.where(side == 0, theirs, mine)
        array = jnp.concatenate([low, high])
        shaped = array.reshape(heads, 2, frames, lats, lons, HD).transpose(1, 2, 3, 4, 0, 5)
        shaped = shaped.reshape(2, frames, lats, lons, width)
        return shaped[0], shaped[1]

    attended, query_out = assembled((done_0, done_1, done_2), (back_out_0, back_out_1, back_out_2))
    theirs_2, ahead_12, attended, query_out = order.passed(theirs_2, ahead_12, attended, query_out)
    ahead_1, ahead_2 = ahead_12[: last - first], ahead_12[last - first :]
    mine = [
        (total(near, twin, 0) + ahead.astype(jnp.float32)).astype(jnp.bfloat16)
        for near, twin, ahead in ((near_0, stay_0, ahead_0), (near_1, stay_1, ahead_1), (near_2, stay_2, ahead_2))
    ]
    key_out, value_out = assembled(mine, (theirs_0, theirs_1, theirs_2))
    return attended, query_out, key_out, value_out


def solution(mesh):
    rows = P("tm", None, "lon", "head")
    return jax.shard_map(
        on_device,
        mesh=mesh,
        in_specs=(rows, rows, rows, rows, P("tm", None, "lon")),
        out_specs=(rows, rows, rows, rows),
        check_vma=False,
    )
```
